128 devices in a mesh: dp: 4 (over x), space: 32 (over z, y, core).
Axes of the slice: x: 4, y: 4, z: 4, core: 2. Of those that a mesh axis runs over, the one named last changes fastest.
Arguments:
- tiles: bfloat16 [4096, 32, 2048], P(('dp', 'space')), may hold values from -6 to 6
- cotangent: bfloat16 [4096, 32, 8192], P(('dp', 'space')), may hold values from -6 to 6
- neighbours: int32 [4096, 8], P(('dp', 'space')), may hold values from -1 to 1023, as said below
- conv_weight: bfloat16 [9, 4096], replicated, may hold values from -0.25 to 0.25
- expand_weight: bfloat16 [64, 256], replicated, may hold values from -0.375 to 0.375
- norm_scale: float32 [64], replicated, may hold values from 0.1 to 1.9
- norm_shift: float32 [64], replicated, may hold values from -3 to 3
Outputs:
- tile_grad: bfloat16 [4096, 32, 2048], P(('dp', 'space'))
- conv_grad: float32 [9, 4096], replicated
- expand_grad: float32 [64, 256], replicated
The draws below stay inside these ranges and needn't reach their ends.
Inputs may be any that keep to these rules, and one draw needn't show every extreme that they name: `neighbours`: each slide's tissue tiles are listed in raster order of a grid of 23 rows and 95 columns; an entry names the tile in that grid direction, -1 where it is background or outside the grid. Relations are mutual. N, W, NW, NE always name an earlier tile and S, E, SW, SE a later one, at most 96 places away in the list; a W entry, when present, is the tile just before and an E entry the tile just after.
All inputs are finite; a program needn't handle non-finite values.
Results may differ from the reference program's by a relative error of at most 0.0049.
Values may be sent and summed in bfloat16 or wider, within the bound.
No kernel may reach another device: no remote copies, remote signals or barrier semaphores. Data moves between devices by JAX's collectives and lax.ppermute only.
A program may use at most 256 MiB of HBM per device.

```python
import math
import jax
import jax.numpy as jnp
import numpy as np
from jax import lax

C = 64
CU = 256
S = 32
TPD = 32
SLIDES = 4
TILES = 1024
GRID_W = 95
GRID_H = 23


grid_moves = ((-1, 0), (1, 0), (0, -1), (0, 1), (-1, -1), (-1, 1), (1, -1), (1, 1))


def slide_links(slide_key):
    grid_cells = GRID_H * GRID_W
    forced = GRID_W + TPD + 1
    optional = jax.random.permutation(slide_key, grid_cells - forced - 2).astype(jnp.int32) + forced
    chosen = optional[:TILES - forced - 2]
    cell_ids = jnp.arange(grid_cells, dtype=jnp.int32)
    tissue = ((cell_ids < forced) | (cell_ids >= grid_cells - 2)).astype(jnp.int32)
    tissue = tissue.at[chosen].set(1)
    tissue_rank = (jnp.cumsum(tissue) - 1).astype(jnp.int32)
    raster_tiles = jnp.argsort(1 - tissue, stable=True)[:TILES].astype(jnp.int32)
    row_index = raster_tiles // GRID_W
    col_index = raster_tiles % GRID_W
    columns = []
    for row_step, col_step in grid_moves:
        target_row = row_index + row_step
        target_col = col_index + col_step
        inside = (target_row >= 0) & (target_row < GRID_H) & (target_col >= 0) & (target_col < GRID_W)
        target = jnp.clip(target_row * GRID_W + target_col, 0, grid_cells - 1)
        columns.append(jnp.where(inside & (tissue[target] == 1), tissue_rank[target], -1))
    return jnp.stack(columns, axis=1).astype(jnp.int32)


def draw_neighbours(key, part):
    slide_lists = [slide_links(jax.random.fold_in(key, slide_index)) for slide_index in range(SLIDES)]
    return jnp.concatenate(slide_lists, axis=0).astype(jnp.int32)


def shard_levels(key, extent, cuts, least, largest):
    def one(axis_at, parts):
        steps = jax.random.uniform(jax.random.fold_in(jax.random.fold_in(key, 6), axis_at), (parts,), jnp.float32, least / len(cuts), largest / len(cuts))
        return jnp.repeat(jnp.exp(steps), extent[axis_at] // parts).reshape((-1,) + (1,) * (len(extent) - axis_at - 1))

    level = one(*cuts[0])
    for cut in cuts[1:]:
        level = level * one(*cut)
    return level


def scatter_about(own_key, extent, width, bound, split=(), held_as=jnp.bfloat16):
    values = jax.random.normal(own_key, extent, jnp.float32) * width
    if len(split) > 0:
        values = shard_levels(own_key, extent, split, -0.22, 0.18) * values
    return jnp.clip(values, min=-bound, max=bound).astype(held_as)


def setup_inputs(seed: int = 0) -> dict:
    seeds = jax.random.split(jax.random.key(seed), 8)
    tiles = scatter_about(seeds[0], (SLIDES * TILES, S, S * C), 1.0, 6.0, ((0, 128),))
    cotangent = scatter_about(seeds[1], (SLIDES * TILES, S, S * CU), 1.0, 6.0, ((0, 128),))
    neighbours = draw_neighbours(jax.random.fold_in(seeds[7], 71), 0)
    conv_weight = scatter_about(seeds[3], (9, C * C), (9 * C) ** -0.5, 0.25)
    expand_weight = scatter_about(seeds[4], (C, CU), CU ** -0.5, 0.375)
    norm_scale = jnp.clip(1.0 + 0.18 * jax.random.normal(seeds[5], (C,), jnp.float32), 0.1, 1.9)
    norm_shift = scatter_about(seeds[6], (C,), 0.5, 3.0, (), jnp.float32)
    return dict(tiles=tiles, cotangent=cotangent, neighbours=neighbours, conv_weight=conv_weight, expand_weight=expand_weight, norm_scale=norm_scale, norm_shift=norm_shift)


early_dirs = np.array([0, 2, 4, 5])
late_dirs = np.array([1, 3, 6, 7])

def edge_parts(features):
    tile_count, tile_side, _, channels = features.shape
    bottom_row = features[:, tile_side - 1].reshape(tile_count, tile_side * channels)
    right_col = features[:, :, tile_side - 1].reshape(tile_count, tile_side * channels)
    top_row = features[:, 0].reshape(tile_count, tile_side * channels)
    left_col = features[:, :, 0].reshape(tile_count, tile_side * channels)
    return (jnp.stack([bottom_row, right_col], axis=1), jnp.stack([top_row, left_col], axis=1))

def assemble(features, early, late, early_ok, late_ok):
    tile_count, tile_side, _, channels = features.shape

    def cycle_piece(strip_rows, present):
        shaped = strip_rows.reshape(tile_count, tile_side, channels)
        return jnp.where(present[:, None, None], shaped, jnp.zeros((), features.dtype))
    north_row = cycle_piece(early[:, 0, 0], early_ok[:, 0])
    west_col = cycle_piece(early[:, 1, 1], early_ok[:, 1])
    north_west = cycle_piece(early[:, 2, 0], early_ok[:, 2])[:, tile_side - 1]
    north_east = cycle_piece(early[:, 3, 0], early_ok[:, 3])[:, 0]
    south_row = cycle_piece(late[:, 0, 0], late_ok[:, 0])
    east_col = cycle_piece(late[:, 1, 1], late_ok[:, 1])
    south_west = cycle_piece(late[:, 2, 0], late_ok[:, 2])[:, tile_side - 1]
    south_east = cycle_piece(late[:, 3, 0], late_ok[:, 3])[:, 0]
    upper_cycle = jnp.concatenate([north_west[:, None], north_row, north_east[:, None]], axis=1)
    middle = jnp.concatenate([west_col[:, :, None], features, east_col[:, :, None]], axis=2)
    lower_cycle = jnp.concatenate([south_west[:, None], south_row, south_east[:, None]], axis=1)
    return jnp.concatenate([upper_cycle[:, None], middle, lower_cycle[:, None]], axis=1)

def pad_slide(features, neighbour_rows):
    earlier_edges, later_edges = edge_parts(features)
    early_index = neighbour_rows[:, early_dirs]
    late_index = neighbour_rows[:, late_dirs]
    early = earlier_edges[jnp.maximum(early_index, 0)]
    late = later_edges[jnp.maximum(late_index, 0)]
    return assemble(features, early, late, early_index >= 0, late_index >= 0)

def convolve(padded, kernel):
    return lax.conv_general_dilated(padded, kernel, (1, 1), 'VALID', dimension_numbers=('NHWC', 'HWIO', 'NHWC'), preferred_element_type=jnp.float32)

def kernel_grad(padded, delta_flat, tile_side, channels):
    kernel_terms = []
    for row_shift in range(3):
        for col_shift in range(3):
            window_cells = padded[:, row_shift:row_shift + tile_side, col_shift:col_shift + tile_side, :].reshape(-1, channels)
            kernel_terms.append(lax.dot_general(window_cells, delta_flat, (((0,), (0,)), ((), ())), preferred_element_type=jnp.float32))
    return jnp.stack(kernel_terms).reshape(9, channels * channels)

def reference(tiles, cotangent, neighbours, conv_weight, expand_weight, norm_scale, norm_shift):
    kernel = conv_weight.reshape(3, 3, C, C)
    flipped = jnp.transpose(jnp.flip(kernel, (0, 1)), (0, 1, 3, 2))
    loss_scale = 1.0 / math.sqrt(SLIDES * TILES * S * S)
    conv_total = jnp.zeros((9, C * C), jnp.float32)
    expand_total = jnp.zeros((C, CU), jnp.float32)
    outputs = []
    for slide_index in range(SLIDES):
        first = slide_index * TILES
        features = tiles[first:first + TILES].reshape(TILES, S, S, C)
        neighbour_rows = neighbours[first:first + TILES]
        padded = pad_slide(features, neighbour_rows)
        conv_out = convolve(padded, kernel)
        pre_act = conv_out * norm_scale + norm_shift
        hidden = jax.nn.silu(pre_act).astype(jnp.bfloat16)
        upstream_in = cotangent[first:first + TILES].reshape(TILES * S * S, CU)
        upstream = lax.dot_general(upstream_in, expand_weight, (((1,), (1,)), ((), ())), preferred_element_type=jnp.float32)
        sigmoid_pre = jax.nn.sigmoid(pre_act)
        conv_delta = (upstream.reshape(pre_act.shape) * sigmoid_pre * (1.0 + pre_act * (1.0 - sigmoid_pre)) * norm_scale).astype(jnp.bfloat16)
        padded_delta = pad_slide(conv_delta, neighbour_rows)
        input_grad = convolve(padded_delta, flipped).astype(jnp.bfloat16)
        outputs.append(input_grad.reshape(TILES, S, S * C))
        conv_total = conv_total + kernel_grad(padded, conv_delta.reshape(-1, C), S, C)
        expand_total = expand_total + lax.dot_general(hidden.reshape(-1, C), upstream_in, (((0,), (0,)), ((), ())), preferred_element_type=jnp.float32)
    return (jnp.concatenate(outputs, axis=0), conv_total * loss_scale, expand_total * loss_scale)
```

```python
import math

import jax
import jax.numpy as jnp
from jax import lax
from jax.experimental import pallas as pl
from jax.experimental.pallas import tpu as pltpu
from jax.sharding import PartitionSpec as P

C = 64
CU = 256
S = 32
REACH = 3
W = S * C
GROUPS = 8
GW = W // GROUPS
KW = 2 * GW
PAIR = 2 * C
PW = W + 2 * PAIR
TB = 4
BF = jnp.bfloat16
F32 = jnp.float32
AXES = ("dp", "space")


def shifted(value, by):
    length = lax.axis_size("space")
    pairs = [(i, i + by) for i in range(length) if 0 <= i + by < length]
    return lax.ppermute(value, "space", pairs)


def one_hot(index, ok, rows):
    place = jnp.where(ok, index, -1)
    return (place[:, None] == lax.broadcasted_iota(jnp.int32, (1, rows), 1)).astype(BF)


def halo(field, neighbours, position):
    count = field.shape[0]
    rows = (REACH + 1) * count

    def side(own, column, sign, names, left_lanes, right_lanes):
        first = jnp.concatenate([own, column], axis=1)
        near = shifted(first, sign)
        far = [shifted(own, sign * d) for d in range(2, REACH + 1)]
        window = jnp.concatenate([own, near[:, :W], *far], axis=0)

        def pick(name, lanes):
            index = neighbours[:, name]
            clipped = jnp.maximum(index, 0)
            place = sign * (position - clipped // count) * count + clipped % count
            chosen = one_hot(place, index >= 0, rows)
            return jnp.dot(chosen, window[:, lanes], preferred_element_type=F32)

        middle, left, right = names
        row = jnp.concatenate(
            [pick(left, slice(W - PAIR, W)), pick(middle, slice(0, W)), pick(right, slice(0, PAIR))],
            axis=1,
        )
        return row, near[:, W:]

    north, west = side(field[:, S - 1], field[count - 1, :, W - PAIR :], 1, (0, 4, 5), None, None)
    south, east = side(field[:, 0], field[0, :, :PAIR], -1, (1, 6, 7), None, None)
    return north, south, west, east


def band(kernel):
    tall = kernel.reshape(3, 3 * C, C)
    columns = [
        jnp.pad(tall, ((0, 0), (C * (j + 1), C * (4 - j)), (0, 0))) for j in range(4)
    ]
    return jnp.concatenate(columns, axis=2).reshape(3 * KW, GW)


def stack_windows(k, field_ref, prev_ref, next_ref, north_ref, south_ref, west_ref, east_ref, nb_ref, lhs_ref):
    step = pl.program_id(0)
    steps = pl.num_programs(0)
    tile = step * TB + k
    if k > 0:
        left = field_ref[k - 1, :, W - PAIR :]
    else:
        left = jnp.where(step == 0, west_ref[...], prev_ref[0])
    if k < TB - 1:
        right = field_ref[k + 1, :, :PAIR]
    else:
        right = jnp.where(step == steps - 1, east_ref[...], next_ref[0])
    left = jnp.where(nb_ref[tile, 2] >= 0, left, jnp.zeros_like(left))
    right = jnp.where(nb_ref[tile, 3] >= 0, right, jnp.zeros_like(right))
    middle = jnp.concatenate([left, field_ref[k], right], axis=1)
    wide = middle.astype(F32)
    place = lax.broadcasted_iota(jnp.int32, (S, PW), 0)
    above = jnp.where(place == 0, north_ref[pl.ds(tile, 1), :], pltpu.roll(wide, 1, 0)).astype(BF)
    below = jnp.where(place == S - 1, south_ref[pl.ds(tile, 1), :], pltpu.roll(wide, S - 1, 0)).astype(BF)
    for a, rows in enumerate((above, middle, below)):
        for g in range(GROUPS):
            at = (k * GROUPS + g) * S
            lhs_ref[at : at + S, a * KW : (a + 1) * KW] = rows[:, g * GW : g * GW + KW]


def forward_kernel(
    nb_ref, field_ref, prev_ref, next_ref, north_ref, south_ref, west_ref, east_ref, cot_ref,
    band_ref, wide_ref, half_scale_ref, half_shift_ref, scale_ref,
    delta_ref, conv_ref, expand_ref, lhs_ref, conv_acc, expand_acc, hidden_ref, stacked_ref,
):
    step = pl.program_id(0)

    @pl.when(step == 0)
    def _():
        conv_acc[...] = jnp.zeros_like(conv_acc)
        expand_acc[...] = jnp.zeros_like(expand_acc)

    per = GROUPS * S
    for k in range(TB):
        stack_windows(k, field_ref, prev_ref, next_ref, north_ref, south_ref, west_ref, east_ref, nb_ref, lhs_ref)
    for k in range(TB):
        rows = slice(k * per, (k + 1) * per)
        conv = jnp.dot(lhs_ref[rows, :], band_ref[...], preferred_element_type=F32)
        cot = jnp.concatenate(
            [cot_ref[k, :, g * 4 * CU : (g + 1) * 4 * CU] for g in range(GROUPS)], axis=0
        )
        up = jnp.dot(cot, wide_ref[...], preferred_element_type=F32)
        half = conv * half_scale_ref[...] + half_shift_ref[...]
        th = jnp.tanh(half)
        s = 0.5 * th + 0.5
        hidden = half * (th + 1.0)
        delta = (up * scale_ref[...] * (s + hidden * (1.0 - s))).astype(BF)
        hidden_ref[rows, :] = hidden.astype(BF)
        stacked_ref[rows, :] = delta
        for g in range(GROUPS):
            delta_ref[k, :, g * GW : (g + 1) * GW] = delta[g * S : (g + 1) * S]
    contract = (((0,), (0,)), ((), ()))
    conv_acc[...] += lax.dot_general(stacked_ref[...], lhs_ref[...], contract, preferred_element_type=F32)
    total = expand_acc[...]
    for j in range(4):
        cot = jnp.concatenate(
            [
                cot_ref[k, :, (g * 4 + j) * CU : (g * 4 + j + 1) * CU]
                for k in range(TB)
                for g in range(GROUPS)
            ],
            axis=0,
        )
        total += lax.dot_general(hidden_ref[:, j * C : (j + 1) * C], cot, contract, preferred_element_type=F32)
    expand_acc[...] = total

    @pl.when(step == pl.num_programs(0) - 1)
    def _():
        expand_ref[...] = expand_acc[...]
        for a in range(3):
            for b in range(3):
                part = jnp.zeros((C, C), F32)
                for j in range(4):
                    lanes = a * KW + C * (j + b + 1)
                    part += conv_acc[j * C : (j + 1) * C, lanes : lanes + C]
                conv_ref[3 * a + b] = part.T


def backward_kernel(
    nb_ref, field_ref, prev_ref, next_ref, north_ref, south_ref, west_ref, east_ref, band_ref, out_ref, lhs_ref
):
    per = GROUPS * S
    for k in range(TB):
        stack_windows(k, field_ref, prev_ref, next_ref, north_ref, south_ref, west_ref, east_ref, nb_ref, lhs_ref)
    for k in range(TB):
        rows = slice(k * per, (k + 1) * per)
        grad = jnp.dot(lhs_ref[rows, :], band_ref[...], preferred_element_type=F32).astype(BF)
        for g in range(GROUPS):
            out_ref[k, :, g * GW : (g + 1) * GW] = grad[g * S : (g + 1) * S]


def field_specs(count):
    last = W // PAIR - 1
    return [
        pl.BlockSpec((TB, S, W), lambda i, nb: (i, 0, 0)),
        pl.BlockSpec((1, S, PAIR), lambda i, nb: (jnp.maximum(i * TB - 1, 0), 0, last)),
        pl.BlockSpec((1, S, PAIR), lambda i, nb: (jnp.minimum(i * TB + TB, count - 1), 0, 0)),
        pl.BlockSpec((count, PW), lambda i, nb: (0, 0)),
        pl.BlockSpec((count, PW), lambda i, nb: (0, 0)),
        pl.BlockSpec((S, PAIR), lambda i, nb: (0, 0)),
        pl.BlockSpec((S, PAIR), lambda i, nb: (0, 0)),
    ]


def whole(*shape):
    return pl.BlockSpec(shape, lambda i, nb: (0,) * len(shape))


def forward(tiles, halos, cotangent, neighbours, bands, wide, half_scale, half_shift, scale):
    count = tiles.shape[0]
    rows = TB * GROUPS * S
    return pl.pallas_call(
        forward_kernel,
        grid_spec=pltpu.PrefetchScalarGridSpec(
            num_scalar_prefetch=1,
            grid=(count // TB,),
            in_specs=[
                *field_specs(count),
                pl.BlockSpec((TB, S, S * CU), lambda i, nb: (i, 0, 0)),
                whole(3 * KW, GW), whole(4 * CU, GW), whole(1, GW), whole(1, GW), whole(1, GW),
            ],
            out_specs=[
                pl.BlockSpec((TB, S, W), lambda i, nb: (i, 0, 0)),
                whole(9, C, C),
                whole(C, CU),
            ],
            scratch_shapes=[
                pltpu.VMEM((rows, 3 * KW), BF),
                pltpu.VMEM((GW, 3 * KW), F32),
                pltpu.VMEM((C, CU), F32),
                pltpu.VMEM((rows, GW), BF),
                pltpu.VMEM((rows, GW), BF),
            ],
        ),
        out_shape=[
            jax.ShapeDtypeStruct((count, S, W), BF),
            jax.ShapeDtypeStruct((9, C, C), F32),
            jax.ShapeDtypeStruct((C, CU), F32),
        ],
        compiler_params=pltpu.CompilerParams(
            dimension_semantics=("arbitrary",), vmem_limit_bytes=48 * 2**20
        ),
        name="forward",
    )(neighbours, tiles, tiles, tiles, *halos, cotangent, bands, wide, half_scale, half_shift, scale)


def backward(delta, halos, neighbours, bands):
    count = delta.shape[0]
    rows = TB * GROUPS * S
    return pl.pallas_call(
        backward_kernel,
        grid_spec=pltpu.PrefetchScalarGridSpec(
            num_scalar_prefetch=1,
            grid=(count // TB,),
            in_specs=[*field_specs(count), whole(3 * KW, GW)],
            out_specs=pl.BlockSpec((TB, S, W), lambda i, nb: (i, 0, 0)),
            scratch_shapes=[pltpu.VMEM((rows, 3 * KW), BF)],
        ),
        out_shape=jax.ShapeDtypeStruct((count, S, W), BF),
        compiler_params=pltpu.CompilerParams(
            dimension_semantics=("arbitrary",), vmem_limit_bytes=48 * 2**20
        ),
        name="backward",
    )(neighbours, delta, delta, delta, *halos, bands)


def swapped(value, move):
    cells = [(x, z, y, c) for x in range(4) for z in range(4) for y in range(4) for c in range(2)]
    number = {cell: i for i, cell in enumerate(cells)}
    return lax.ppermute(value, AXES, [(number[cell], number[move(cell)]) for cell in cells])


def flip(axis, second):
    def move(cell):
        there = list(cell)
        there[axis] = 3 - cell[axis] if second else cell[axis] ^ 1
        return tuple(there)

    return move


def summed(value):
    half = value.shape[0] // 2
    even = lax.axis_index("space") % 2 == 0
    low, high = value[:half], value[half:]
    part = jnp.where(even, low, high) + swapped(jnp.where(even, high, low), flip(3, False))
    for axis in range(3):
        for second in (False, True):
            part = part + swapped(part, flip(axis, second))
    other = swapped(part, flip(3, False))
    return jnp.concatenate([jnp.where(even, part, other), jnp.where(even, other, part)], axis=0)


def local(tiles, cotangent, neighbours, conv_weight, expand_weight, norm_scale, norm_shift):
    count = tiles.shape[0]
    position = lax.axis_index("space")
    kernel = conv_weight.reshape(3, 3, C, C)
    flipped = jnp.transpose(jnp.flip(kernel, (0, 1)), (0, 1, 3, 2))
    turned = expand_weight.T
    wide = jnp.concatenate([jnp.pad(turned, ((CU * j, CU * (3 - j)), (0, 0))) for j in range(4)], axis=1)
    scale = jnp.tile(norm_scale, 4)[None]
    half_shift = 0.5 * jnp.tile(norm_shift, 4)[None]
    delta, conv_part, expand_part = forward(
        tiles, halo(tiles, neighbours, position), cotangent, neighbours, band(kernel), wide, 0.5 * scale, half_shift, scale
    )
    cells = lax.axis_size("dp") * lax.axis_size("space") * count * S * S
    part = jnp.concatenate([conv_part.reshape(9 * 32, 2 * C), expand_part.reshape(2 * C, 2 * C)], axis=0)
    total = summed(part) * (1.0 / math.sqrt(cells))
    grad = backward(delta, halo(delta, neighbours, position), neighbours, band(flipped))
    return grad, total[: 9 * 32].reshape(9, C * C), total[9 * 32 :].reshape(C, CU)


def solution(mesh):
    placed = (P(AXES, None, None), P(AXES, None, None), P(AXES, None), P(), P(), P(), P())
    return jax.shard_map(
        local,
        mesh=mesh,
        in_specs=placed,
        out_specs=(P(AXES, None, None), P(), P()),
        check_vma=False,
    )
```

```python
import functools
import math

import jax
import jax.numpy as jnp
from jax import lax
from jax.experimental import pallas as pl
from jax.experimental.pallas import tpu as pltpu
from jax.sharding import PartitionSpec as P

C = 64
CU = 256
S = 32
REACH = 3
W = S * C
GROUPS = 8
GW = W // GROUPS
KW = 2 * GW
PAIR = 2 * C
PW = W + 2 * PAIR
TB = 4
PIECES = 4
BF = jnp.bfloat16
F32 = jnp.float32
AXES = ("dp", "space")


def shifted(value, by):
    length = lax.axis_size("space")
    pairs = [(i, i + by) for i in range(length) if 0 <= i + by < length]
    return lax.ppermute(value, "space", pairs)


def one_hot(index, ok, rows):
    place = jnp.where(ok, index, -1)
    return (place[:, None] == lax.broadcasted_iota(jnp.int32, (1, rows), 1)).astype(BF)


def halo_near(down, up):
    return shifted(down, 1), shifted(up, -1)


def halo_far(down, up, near):
    return shifted(jnp.concatenate([down, near[0]], axis=0), 2), shifted(jnp.concatenate([up, near[1]], axis=0), -2)


def halo(down, up, near, far, neighbours, position):
    count = down.shape[0]
    rows = (REACH + 1) * count

    def side(own, near, far, sign, names):
        window = jnp.concatenate([own, near, far], axis=0)

        def pick(name, lanes):
            index = neighbours[:, name]
            clipped = jnp.maximum(index, 0)
            place = sign * (position - clipped // count) * count + clipped % count
            chosen = one_hot(place, index >= 0, rows)
            return jnp.dot(chosen, window[:, lanes], preferred_element_type=F32)

        middle, left, right = names
        row = jnp.concatenate(
            [pick(left, slice(W - PAIR, W)), pick(middle, slice(0, W)), pick(right, slice(0, PAIR))],
            axis=1,
        )
        return row, near[:, W:]

    north, west = side(down, near[0], far[0], 1, (0, 4, 5))
    south, east = side(up, near[1], far[1], -1, (1, 6, 7))
    return north, south, west, east


def band(kernel):
    tall = kernel.reshape(3, 3 * C, C)
    columns = [
        jnp.pad(tall, ((0, 0), (C * (j + 1), C * (4 - j)), (0, 0))) for j in range(4)
    ]
    return jnp.concatenate(columns, axis=2).reshape(3 * KW, GW)


def store_taps(lhs_ref, at, taps):
    for a, rows in enumerate(taps):
        for g in range(GROUPS):
            lhs_ref[at + g * S : at + (g + 1) * S, a * KW : (a + 1) * KW] = rows[:, g * GW : g * GW + KW]


def kept(ok, value):
    return jnp.where(ok, value, jnp.zeros_like(value))


def with_halo(wide, north, south):
    place = lax.broadcasted_iota(jnp.int32, wide.shape, 0)
    above = jnp.where(place == 0, north, pltpu.roll(wide, 1, 0)).astype(BF)
    below = jnp.where(place == S - 1, south, pltpu.roll(wide, S - 1, 0)).astype(BF)
    return above, wide.astype(BF), below


def activate(conv, up, half_scale, half_shift, scale):
    half = conv * half_scale + half_shift
    th = jnp.tanh(half)
    s = 0.5 * th + 0.5
    hidden = half * (th + 1.0)
    return hidden, up * scale * (s + hidden * (1.0 - s))


CONTRACT = (((0,), (0,)), ((), ()))


def add_conv(acc_ref, taps, delta):
    acc_ref[...] += lax.dot_general(taps, delta, CONTRACT, preferred_element_type=F32)


def finish_conv(acc_ref, before_ref, out_ref):
    for a in range(3):
        for b in range(3):
            part = before_ref[3 * a + b]
            for j in range(4):
                at = a * KW + C * (j + b + 1)
                part += acc_ref[at : at + C, j * C : (j + 1) * C]
            out_ref[3 * a + b] = part


def forward_kernel(
    base, nb_ref, field_ref, prev_ref, next_ref, cot_ref, band_ref, wide_ref, half_scale_ref, half_shift_ref, scale_ref,
    conv_in_ref, expand_in_ref, *rest,
):
    delta_ref, rows_ref, cot_rows_ref, conv_ref, expand_ref, lhs_ref, conv_acc, expand_acc, hidden_ref, stacked_ref = rest[-10:]
    step = pl.program_id(0)
    count = nb_ref.shape[0]

    @pl.when(step == 0)
    def _():
        conv_acc[...] = jnp.zeros_like(conv_acc)
        expand_acc[...] = expand_in_ref[...]

    per = GROUPS * S
    for k in range(TB):
        tile = (step + base) * TB + k
        left = field_ref[k - 1, :, W - PAIR :] if k > 0 else prev_ref[0]
        right = field_ref[k + 1, :, :PAIR] if k < TB - 1 else next_ref[0]
        left = kept(nb_ref[tile, 2] >= 0, left)
        right = kept(nb_ref[tile, 3] >= 0, right)
        middle = jnp.concatenate([left, field_ref[k], right], axis=1)
        wide = middle.astype(F32)
        store_taps(
            lhs_ref, k * per, (pltpu.roll(wide, 1, 0).astype(BF), middle, pltpu.roll(wide, S - 1, 0).astype(BF))
        )
        place = step * TB + k
        for r, at in enumerate((0, 1, S - 2, S - 1)):
            rows_ref[r, pl.ds(place, 1), :] = wide[at : at + 1]
        cot_rows_ref[0, pl.ds(place, 1), :] = cot_ref[k, :16].astype(F32)[:1]
        cot_rows_ref[1, pl.ds(place, 1), :] = cot_ref[k, 16:].astype(F32)[15:]
    inside = lax.broadcasted_iota(jnp.int32, (per, GW), 0) & (S - 1)
    inside = (inside > 0) & (inside < S - 1)
    for k in range(TB):
        tile = (step + base) * TB + k
        rows = slice(k * per, (k + 1) * per)
        conv = jnp.dot(lhs_ref[rows, :], band_ref[...], preferred_element_type=F32)
        cot = jnp.concatenate(
            [cot_ref[k, :, g * 4 * CU : (g + 1) * 4 * CU] for g in range(GROUPS)], axis=0
        )
        up = jnp.dot(cot, wide_ref[...], preferred_element_type=F32)
        hidden, delta = activate(conv, up, half_scale_ref[...], half_shift_ref[...], scale_ref[...])
        ok = inside
        if k in (0, TB - 1):
            ok = inside & ((tile > 0) & (tile < count - 1))
        hidden_ref[rows, :] = kept(ok, hidden).astype(BF)
        delta = kept(ok, delta).astype(BF)
        stacked_ref[rows, :] = delta
        for g in range(GROUPS):
            delta_ref[k, :, g * GW : (g + 1) * GW] = delta[g * S : (g + 1) * S]
    add_conv(conv_acc, lhs_ref[...], stacked_ref[...])
    total = expand_acc[...]
    for j in range(4):
        cot = jnp.concatenate(
            [
                cot_ref[k, :, (g * 4 + j) * CU : (g * 4 + j + 1) * CU]
                for k in range(TB)
                for g in range(GROUPS)
            ],
            axis=0,
        )
        total += lax.dot_general(hidden_ref[:, j * C : (j + 1) * C], cot, CONTRACT, preferred_element_type=F32)
    expand_acc[...] = total

    @pl.when(step == pl.num_programs(0) - 1)
    def _():
        expand_ref[...] = expand_acc[...]
        finish_conv(conv_acc, conv_in_ref, conv_ref)


def edge_kernel(
    nb_ref, tile_ref, prev_ref, next_ref, cot_ref, rows_a_ref, rows_b_ref, cot_a_ref, cot_b_ref,
    north_ref, south_ref, west_ref, east_ref, band_ref, wide_ref, half_scale_ref, half_shift_ref, scale_ref,
    conv_in_ref, expand_in_ref, delta_in_ref,
    delta_ref, up_ref, down_ref, up_own_ref, down_own_ref, conv_ref, expand_ref,
    lhs_ref, cots_ref, conv_acc, expand_acc,
):
    step = pl.program_id(0)
    count = nb_ref.shape[0]
    west = kept(nb_ref[0, 2] >= 0, west_ref[...].astype(F32))
    east = kept(nb_ref[count - 1, 3] >= 0, east_ref[...].astype(F32))

    @pl.when(step == 0)
    def _():
        conv_acc[...] = jnp.zeros_like(conv_acc)
        expand_acc[...] = expand_in_ref[...]

    @pl.when(step < 2)
    def _():
        first = step == 0
        left = jnp.where(first, west, kept(nb_ref[count - 1, 2] >= 0, prev_ref[0].astype(F32)))
        right = jnp.where(first, kept(nb_ref[0, 3] >= 0, next_ref[0].astype(F32)), east)
        wide = jnp.concatenate([left, tile_ref[0].astype(F32), right], axis=1)
        north = jnp.where(first, north_ref[:1], north_ref[count - 1 :])
        south = jnp.where(first, south_ref[:1], south_ref[count - 1 :])
        store_taps(lhs_ref, 0, with_halo(wide, north, south))
        for g in range(GROUPS):
            cots_ref[g * S : (g + 1) * S, :] = cot_ref[0, :, g * 4 * CU : (g + 1) * 4 * CU]

    top = step == 2

    @pl.when(step >= 2)
    def _():
        tile_at = lax.broadcasted_iota(jnp.int32, (count, PAIR), 0)

        def row(r, at):
            found = jnp.concatenate([rows_a_ref[r], rows_b_ref[r]], axis=0)
            left = jnp.where(tile_at == 0, west[at : at + 1], found[:, :PAIR])
            right = jnp.where(tile_at == count - 1, east[at : at + 1], found[:, PW - PAIR :])
            return jnp.concatenate([left, found[:, PAIR : PW - PAIR], right], axis=1)

        edge = jnp.where(top, row(0, 0), row(3, S - 1))
        inner = jnp.where(top, row(1, 1), row(2, S - 2))
        above = jnp.where(top, north_ref[...], inner)
        below = jnp.where(top, inner, south_ref[...])
        store_taps(lhs_ref, 0, (above.astype(BF), edge.astype(BF), below.astype(BF)))
        cot = jnp.where(
            top,
            jnp.concatenate([cot_a_ref[0], cot_b_ref[0]], axis=0),
            jnp.concatenate([cot_a_ref[1], cot_b_ref[1]], axis=0),
        ).astype(BF)
        for g in range(GROUPS):
            cots_ref[g * S : (g + 1) * S, :] = cot[:, g * 4 * CU : (g + 1) * 4 * CU]

    conv = jnp.dot(lhs_ref[...], band_ref[...], preferred_element_type=F32)
    up = jnp.dot(cots_ref[...], wide_ref[...], preferred_element_type=F32)
    hidden, delta = activate(conv, up, half_scale_ref[...], half_shift_ref[...], scale_ref[...])
    at = lax.broadcasted_iota(jnp.int32, hidden.shape, 0) & (S - 1)
    ok = ((at > 0) & (at < count - 1)) | (step < 2)
    rounded = delta.astype(BF)
    hidden = kept(ok, hidden).astype(BF)
    add_conv(conv_acc, lhs_ref[...], kept(ok, delta).astype(BF))
    for j in range(4):
        expand_acc[...] += lax.dot_general(
            hidden[:, j * C : (j + 1) * C], cots_ref[:, j * CU : (j + 1) * CU], CONTRACT, preferred_element_type=F32
        )

    @pl.when(step < 2)
    def _():
        for g in range(GROUPS):
            delta_ref[0, :, g * GW : (g + 1) * GW] = rounded[g * S : (g + 1) * S]

    @pl.when(step == 0)
    def _():
        up_ref[:, W:] = rounded[:S, :PAIR]

    @pl.when(step == 1)
    def _():
        down_ref[:, W:] = rounded[(GROUPS - 1) * S :, GW - PAIR :]

    def rows_out(sent_ref, own_ref):
        for g in range(GROUPS):
            sent_ref[:, g * GW : (g + 1) * GW] = rounded[g * S : (g + 1) * S]
            own_ref[:, g * GW : (g + 1) * GW] = rounded[g * S : (g + 1) * S].astype(F32)

    @pl.when(step == 2)
    def _():
        rows_out(up_ref, up_own_ref)

    @pl.when(step == 3)
    def _():
        rows_out(down_ref, down_own_ref)
        expand_ref[...] = expand_acc[...]
        finish_conv(conv_acc, conv_in_ref, conv_ref)


def backward_kernel(
    base, nb_ref, field_ref, prev_ref, next_ref, north_ref, south_ref, west_ref, east_ref, top_ref, bottom_ref, band_ref, *rest
):
    out_ref, lhs_ref = rest[-2:]
    step = pl.program_id(0) + base
    count = nb_ref.shape[0]
    per = GROUPS * S

    def mended(value, tile, lanes):
        place = lax.broadcasted_iota(jnp.int32, value.shape, 0)
        value = jnp.where(place == 0, top_ref[pl.ds(tile, 1), :][:, lanes], value.astype(F32))
        return jnp.where(place == S - 1, bottom_ref[pl.ds(tile, 1), :][:, lanes], value)

    for k in range(TB):
        tile = step * TB + k
        left = field_ref[k - 1, :, W - PAIR :] if k > 0 else prev_ref[0]
        right = field_ref[k + 1, :, :PAIR] if k < TB - 1 else next_ref[0]
        left = mended(left, jnp.maximum(tile - 1, 0), slice(W - PAIR, W))
        right = mended(right, jnp.minimum(tile + 1, count - 1), slice(0, PAIR))
        if k == 0:
            left = jnp.where(tile == 0, west_ref[...].astype(F32), left)
        if k == TB - 1:
            right = jnp.where(tile == count - 1, east_ref[...].astype(F32), right)
        left = kept(nb_ref[tile, 2] >= 0, left)
        right = kept(nb_ref[tile, 3] >= 0, right)
        wide = jnp.concatenate([left, mended(field_ref[k], tile, slice(0, W)), right], axis=1)
        taps = with_halo(wide, north_ref[pl.ds(tile, 1), :], south_ref[pl.ds(tile, 1), :])
        store_taps(lhs_ref, k * per, taps)
    for k in range(TB):
        rows = slice(k * per, (k + 1) * per)
        grad = jnp.dot(lhs_ref[rows, :], band_ref[...], preferred_element_type=F32).astype(BF)
        for g in range(GROUPS):
            out_ref[k, :, g * GW : (g + 1) * GW] = grad[g * S : (g + 1) * S]


def field_specs(count, base):
    last = W // PAIR - 1
    return [
        pl.BlockSpec((TB, S, W), lambda i, nb: (i + base, 0, 0)),
        pl.BlockSpec((1, S, PAIR), lambda i, nb: (jnp.maximum((i + base) * TB - 1, 0), 0, last)),
        pl.BlockSpec((1, S, PAIR), lambda i, nb: (jnp.minimum((i + base) * TB + TB, count - 1), 0, 0)),
    ]


def whole(*shape):
    return pl.BlockSpec(shape, lambda i, nb: (0,) * len(shape))


ANY = pl.BlockSpec(memory_space=pl.ANY)
PARAMS = pltpu.CompilerParams(dimension_semantics=("arbitrary",), vmem_limit_bytes=44 * 2**20)
CONSTANTS = ((3 * KW, GW), (4 * CU, GW), (1, GW), (1, GW), (1, GW))
GRADS = ((9, C, C), (C, CU))


def halo_specs(count):
    return [whole(count, PW), whole(count, PW), whole(S, PAIR), whole(S, PAIR)]


def forward(tiles, cotangent, neighbours, constants, base, steps, grads, before=None):
    count = tiles.shape[0]
    rows = TB * GROUPS * S
    more = [] if before is None else [before]
    return pl.pallas_call(
        functools.partial(forward_kernel, base),
        grid_spec=pltpu.PrefetchScalarGridSpec(
            num_scalar_prefetch=1,
            grid=(steps,),
            in_specs=[
                *field_specs(count, base),
                pl.BlockSpec((TB, S, S * CU), lambda i, nb: (i + base, 0, 0)),
                *[whole(*shape) for shape in CONSTANTS + GRADS],
                *[ANY for _ in more],
            ],
            out_specs=[
                pl.BlockSpec((TB, S, W), lambda i, nb: (i + base, 0, 0)),
                whole(4, steps * TB, PW),
                whole(2, steps * TB, S * CU),
                *[whole(*shape) for shape in GRADS],
            ],
            scratch_shapes=[
                pltpu.VMEM((rows, 3 * KW), BF),
                pltpu.VMEM((3 * KW, GW), F32),
                pltpu.VMEM((C, CU), F32),
                pltpu.VMEM((rows, GW), BF),
                pltpu.VMEM((rows, GW), BF),
            ],
        ),
        out_shape=[
            jax.ShapeDtypeStruct((count, S, W), BF),
            jax.ShapeDtypeStruct((4, steps * TB, PW), F32),
            jax.ShapeDtypeStruct((2, steps * TB, S * CU), F32),
            *[jax.ShapeDtypeStruct(shape, F32) for shape in GRADS],
        ],
        input_output_aliases={12: 0} if more else {},
        compiler_params=PARAMS,
        cost_estimate=pl.CostEstimate(flops=steps * 2**32, bytes_accessed=steps * 3 * 2**20, transcendentals=0),
        name=f"forward_{base}",
    )(neighbours, tiles, tiles, tiles, cotangent, *constants, *grads, *more)


def edges(tiles, cotangent, neighbours, kept_rows, halos, constants, grads, delta):
    count = tiles.shape[0]
    ends = count - 1
    (rows_a, cot_a), (rows_b, cot_b) = kept_rows
    own = (count, W)
    sent = (count, W + PAIR)
    return pl.pallas_call(
        edge_kernel,
        grid_spec=pltpu.PrefetchScalarGridSpec(
            num_scalar_prefetch=1,
            grid=(4,),
            in_specs=[
                pl.BlockSpec((1, S, W), lambda i, nb: (ends * jnp.minimum(i, 1), 0, 0)),
                pl.BlockSpec((1, S, PAIR), lambda i, nb: (ends - 1, 0, W // PAIR - 1)),
                pl.BlockSpec((1, S, PAIR), lambda i, nb: (1, 0, 0)),
                pl.BlockSpec((1, S, S * CU), lambda i, nb: (ends * jnp.minimum(i, 1), 0, 0)),
                *[whole(*value.shape) for value in (rows_a, rows_b, cot_a, cot_b)],
                *halo_specs(count),
                *[whole(*shape) for shape in CONSTANTS + GRADS],
                ANY,
            ],
            out_specs=[
                pl.BlockSpec((1, S, W), lambda i, nb: (ends * jnp.minimum(i, 1), 0, 0)),
                whole(*sent), whole(*sent), whole(*own), whole(*own),
                *[whole(*shape) for shape in GRADS],
            ],
            scratch_shapes=[
                pltpu.VMEM((GROUPS * S, 3 * KW), BF),
                pltpu.VMEM((GROUPS * S, 4 * CU), BF),
                pltpu.VMEM((3 * KW, GW), F32),
                pltpu.VMEM((C, CU), F32),
            ],
        ),
        out_shape=[
            jax.ShapeDtypeStruct((count, S, W), BF),
            jax.ShapeDtypeStruct(sent, BF),
            jax.ShapeDtypeStruct(sent, BF),
            jax.ShapeDtypeStruct(own, F32),
            jax.ShapeDtypeStruct(own, F32),
            *[jax.ShapeDtypeStruct(shape, F32) for shape in GRADS],
        ],
        input_output_aliases={20: 0},
        compiler_params=PARAMS,
        cost_estimate=pl.CostEstimate(flops=2**33, bytes_accessed=2**22, transcendentals=0),
        name="edges",
    )(neighbours, tiles, tiles, tiles, cotangent, rows_a, rows_b, cot_a, cot_b, *halos, *constants, *grads, delta)


def backward(delta, halos, own, neighbours, bands, base, steps, before=None):
    count = delta.shape[0]
    rows = TB * GROUPS * S
    more = [] if before is None else [before]
    return pl.pallas_call(
        functools.partial(backward_kernel, base),
        grid_spec=pltpu.PrefetchScalarGridSpec(
            num_scalar_prefetch=1,
            grid=(steps,),
            in_specs=[
                *field_specs(count, base), *halo_specs(count), whole(count, W), whole(count, W), whole(3 * KW, GW),
                *[ANY for _ in more],
            ],
            out_specs=pl.BlockSpec((TB, S, W), lambda i, nb: (i + base, 0, 0)),
            scratch_shapes=[pltpu.VMEM((rows, 3 * KW), BF)],
        ),
        out_shape=jax.ShapeDtypeStruct((count, S, W), BF),
        input_output_aliases={11: 0} if more else {},
        compiler_params=PARAMS,
        cost_estimate=pl.CostEstimate(flops=steps * 2**31, bytes_accessed=steps * 2**20, transcendentals=0),
        name=f"backward_{base}",
    )(neighbours, delta, delta, delta, *halos, *own, bands, *more)


def swapped(value, move):
    cells = [(x, z, y, c) for x in range(4) for z in range(4) for y in range(4) for c in range(2)]
    number = {cell: i for i, cell in enumerate(cells)}
    return lax.ppermute(value, AXES, [(number[cell], number[move(cell)]) for cell in cells])


def flip(axis, second):
    def move(cell):
        there = list(cell)
        there[axis] = 3 - cell[axis] if second else cell[axis] ^ 1
        return tuple(there)

    return move


def tied(*values):
    return lax.optimization_barrier(values)


def local(tiles, cotangent, neighbours, conv_weight, expand_weight, norm_scale, norm_shift):
    count = tiles.shape[0]
    position = lax.axis_index("space")
    kernel = conv_weight.reshape(3, 3, C, C)
    flipped = jnp.transpose(jnp.flip(kernel, (0, 1)), (0, 1, 3, 2))
    turned = expand_weight.T
    wide = jnp.concatenate([jnp.pad(turned, ((CU * j, CU * (3 - j)), (0, 0))) for j in range(4)], axis=1)
    scale = jnp.tile(norm_scale, 4)[None]
    half_shift = 0.5 * jnp.tile(norm_shift, 4)[None]
    constants = (band(kernel), wide, 0.5 * scale, half_shift, scale)
    down = jnp.concatenate([tiles[:, S - 1], tiles[count - 1, :, W - PAIR :]], axis=1)
    up = jnp.concatenate([tiles[:, 0], tiles[0, :, :PAIR]], axis=1)
    blocks = count // TB
    early = blocks // 2

    near = halo_near(down, up)
    grads = tuple(jnp.zeros(shape, F32) for shape in GRADS)
    delta, *first_rows, conv_part, expand_part = forward(tiles, cotangent, neighbours, constants, 0, early, grads)
    near, delta = tied(near, delta)
    far = halo_far(down, up, near)
    delta, *last_rows, conv_part, expand_part = forward(
        tiles, cotangent, neighbours, constants, early, blocks - early, (conv_part, expand_part), delta
    )
    far, delta = tied(far, delta)
    halos = halo(down, up, near, far, neighbours, position)
    delta, up, down, top, bottom, conv_part, expand_part = edges(
        tiles, cotangent, neighbours, (first_rows, last_rows), halos, constants, (conv_part, expand_part), delta
    )

    part = jnp.concatenate([conv_part.reshape(9 * 32, 2 * C), expand_part.reshape(2 * C, 2 * C)], axis=0)
    half = part.shape[0] // 2
    even = lax.axis_index("space") % 2 == 0
    low, high = part[:half], part[half:]
    near = halo_near(down, up)
    other = swapped(jnp.where(even, high, low), flip(3, False))
    near, other = tied(near, other)
    part = jnp.where(even, low, high) + other
    far = halo_far(down, up, near)
    back = band(flipped)
    grad = None
    counts = [blocks * (i + 1) // PIECES - blocks * i // PIECES for i in range(PIECES)]
    halos = None
    for turn in range(6):
        other = swapped(part, flip(turn // 2, turn % 2 == 1))
        piece = turn - (6 - PIECES)
        if piece >= 0:
            if halos is None:
                halos = halo(down, up, near, far, neighbours, position)
            grad = backward(delta, halos, (top, bottom), neighbours, back, sum(counts[:piece]), counts[piece], grad)
            other, grad = tied(other, grad)
        part = part + other
        if grad is not None:
            part, grad = tied(part, grad)
        elif turn == 5 - PIECES:
            part, far = tied(part, far)
    other = swapped(part, flip(3, False))
    total = jnp.concatenate([jnp.where(even, part, other), jnp.where(even, other, part)], axis=0)
    cells = lax.axis_size("dp") * lax.axis_size("space") * count * S * S
    total = total * (1.0 / math.sqrt(cells))
    return grad, total[: 9 * 32].reshape(9, C * C), total[9 * 32 :].reshape(C, CU)


def solution(mesh):
    placed = (P(AXES, None, None), P(AXES, None, None), P(AXES, None), P(), P(), P(), P())
    return jax.shard_map(
        local,
        mesh=mesh,
        in_specs=placed,
        out_specs=(P(AXES, None, None), P(), P()),
        check_vma=False,
    )
```

```python
import functools
import math

import jax
import jax.numpy as jnp
from jax import lax
from jax.experimental import pallas as pl
from jax.experimental.pallas import tpu as pltpu
from jax.sharding import PartitionSpec as P

C = 64
CU = 256
S = 32
REACH = 3
W = S * C
GROUPS = 8
GW = W // GROUPS
KW = 2 * GW
PAIR = 2 * C
PW = W + 2 * PAIR
TB = 4
PIECES = 4
BF = jnp.bfloat16
F32 = jnp.float32
AXES = ("dp", "space")


def shifted(value, by):
    length = lax.axis_size("space")
    pairs = [(i, i + by) for i in range(length) if 0 <= i + by < length]
    return lax.ppermute(value, "space", pairs)


def one_hot(index, ok, rows):
    place = jnp.where(ok, index, -1)
    return (place[:, None] == lax.broadcasted_iota(jnp.int32, (1, rows), 1)).astype(BF)


def halo_near(down, up):
    return shifted(down, 1), shifted(up, -1)


def halo_far(down, up, near):
    return shifted(jnp.concatenate([down, near[0]], axis=0), 2), shifted(jnp.concatenate([up, near[1]], axis=0), -2)


def halo(down, up, near, far, neighbours, position):
    count = down.shape[0]
    rows = (REACH + 1) * count

    def side(own, near, far, sign, names):
        window = jnp.concatenate([own, near, far], axis=0)

        def pick(name, lanes):
            index = neighbours[:, name]
            clipped = jnp.maximum(index, 0)
            place = sign * (position - clipped // count) * count + clipped % count
            chosen = one_hot(place, index >= 0, rows)
            return jnp.dot(chosen, window[:, lanes], preferred_element_type=F32)

        middle, left, right = names
        row = jnp.concatenate(
            [pick(left, slice(W - PAIR, W)), pick(middle, slice(0, W)), pick(right, slice(0, PAIR))],
            axis=1,
        )
        return row, near[:, W:]

    north, west = side(down, near[0], far[0], 1, (0, 4, 5))
    south, east = side(up, near[1], far[1], -1, (1, 6, 7))
    return north, south, west, east


def band(kernel):
    tall = kernel.reshape(3, 3 * C, C)
    columns = [
        jnp.pad(tall, ((0, 0), (C * (j + 1), C * (4 - j)), (0, 0))) for j in range(4)
    ]
    return jnp.concatenate(columns, axis=2).reshape(3 * KW, GW)


def store_taps(lhs_ref, at, taps):
    for a, rows in enumerate(taps):
        for g in range(GROUPS):
            lhs_ref[at + g * S : at + (g + 1) * S, a * KW : (a + 1) * KW] = rows[:, g * GW : g * GW + KW]


def kept(ok, value):
    return jnp.where(ok, value, jnp.zeros_like(value))


def with_halo(wide, north, south):
    place = lax.broadcasted_iota(jnp.int32, wide.shape, 0)
    above = jnp.where(place == 0, north, pltpu.roll(wide, 1, 0)).astype(BF)
    below = jnp.where(place == S - 1, south, pltpu.roll(wide, S - 1, 0)).astype(BF)
    return above, wide.astype(BF), below


def activate(conv, up, half_scale, half_shift, scale):
    half = conv * half_scale + half_shift
    th = jnp.tanh(half)
    s = 0.5 * th + 0.5
    hidden = half * (th + 1.0)
    return hidden, up * scale * (s + hidden * (1.0 - s))


CONTRACT = (((0,), (0,)), ((), ()))


def add_conv(acc_ref, taps, delta):
    acc_ref[...] += lax.dot_general(taps, delta, CONTRACT, preferred_element_type=F32)


def finish_conv(acc_ref, before_ref, out_ref):
    for a in range(3):
        for b in range(3):
            part = before_ref[3 * a + b]
            for j in range(4):
                at = a * KW + C * (j + b + 1)
                part += acc_ref[at : at + C, j * C : (j + 1) * C]
            out_ref[3 * a + b] = part


def forward_kernel(
    base, nb_ref, field_ref, prev_ref, next_ref, cot_ref, band_ref, wide_ref, half_scale_ref, half_shift_ref, scale_ref,
    conv_in_ref, expand_in_ref, *rest,
):
    delta_ref, rows_ref, cot_rows_ref, conv_ref, expand_ref, lhs_ref, conv_acc, expand_acc, hidden_ref, stacked_ref = rest[-10:]
    step = pl.program_id(0)
    count = nb_ref.shape[0]

    @pl.when(step == 0)
    def _():
        conv_acc[...] = jnp.zeros_like(conv_acc)
        expand_acc[...] = expand_in_ref[...]

    per = GROUPS * S
    for k in range(TB):
        tile = (step + base) * TB + k
        left = field_ref[k - 1, :, W - PAIR :] if k > 0 else prev_ref[0]
        right = field_ref[k + 1, :, :PAIR] if k < TB - 1 else next_ref[0]
        left = kept(nb_ref[tile, 2] >= 0, left)
        right = kept(nb_ref[tile, 3] >= 0, right)
        middle = jnp.concatenate([left, field_ref[k], right], axis=1)
        wide = middle.astype(F32)
        store_taps(
            lhs_ref, k * per, (pltpu.roll(wide, 1, 0).astype(BF), middle, pltpu.roll(wide, S - 1, 0).astype(BF))
        )
        place = step * TB + k
        for r, at in enumerate((0, 1, S - 2, S - 1)):
            rows_ref[r, pl.ds(place, 1), :] = wide[at : at + 1]
        cot_rows_ref[0, pl.ds(place, 1), :] = cot_ref[k, :16].astype(F32)[:1]
        cot_rows_ref[1, pl.ds(place, 1), :] = cot_ref[k, 16:].astype(F32)[15:]
    inside = lax.broadcasted_iota(jnp.int32, (per, GW), 0) & (S - 1)
    inside = (inside > 0) & (inside < S - 1)
    for k in range(TB):
        tile = (step + base) * TB + k
        rows = slice(k * per, (k + 1) * per)
        conv = jnp.dot(lhs_ref[rows, :], band_ref[...], preferred_element_type=F32)
        cot = jnp.concatenate(
            [cot_ref[k, :, g * 4 * CU : (g + 1) * 4 * CU] for g in range(GROUPS)], axis=0
        )
        up = jnp.dot(cot, wide_ref[...], preferred_element_type=F32)
        hidden, delta = activate(conv, up, half_scale_ref[...], half_shift_ref[...], scale_ref[...])
        ok = inside
        if k in (0, TB - 1):
            ok = inside & ((tile > 0) & (tile < count - 1))
        hidden_ref[rows, :] = kept(ok, hidden).astype(BF)
        delta = kept(ok, delta).astype(BF)
        stacked_ref[rows, :] = delta
        for g in range(GROUPS):
            delta_ref[k, :, g * GW : (g + 1) * GW] = delta[g * S : (g + 1) * S]
    add_conv(conv_acc, lhs_ref[...], stacked_ref[...])
    total = expand_acc[...]
    for j in range(4):
        cot = jnp.concatenate(
            [
                cot_ref[k, :, (g * 4 + j) * CU : (g * 4 + j + 1) * CU]
                for k in range(TB)
                for g in range(GROUPS)
            ],
            axis=0,
        )
        total += lax.dot_general(hidden_ref[:, j * C : (j + 1) * C], cot, CONTRACT, preferred_element_type=F32)
    expand_acc[...] = total

    @pl.when(step == pl.num_programs(0) - 1)
    def _():
        expand_ref[...] = expand_acc[...]
        finish_conv(conv_acc, conv_in_ref, conv_ref)


def edge_kernel(
    nb_ref, tile_ref, prev_ref, next_ref, cot_ref, rows_a_ref, rows_b_ref, cot_a_ref, cot_b_ref,
    north_ref, south_ref, west_ref, east_ref, band_ref, wide_ref, half_scale_ref, half_shift_ref, scale_ref,
    conv_in_ref, expand_in_ref, delta_in_ref,
    delta_ref, up_ref, down_ref, up_own_ref, down_own_ref, conv_ref, expand_ref,
    lhs_ref, cots_ref, conv_acc, expand_acc,
):
    step = pl.program_id(0)
    count = nb_ref.shape[0]
    west = kept(nb_ref[0, 2] >= 0, west_ref[...].astype(F32))
    east = kept(nb_ref[count - 1, 3] >= 0, east_ref[...].astype(F32))

    @pl.when(step == 0)
    def _():
        conv_acc[...] = jnp.zeros_like(conv_acc)
        expand_acc[...] = expand_in_ref[...]

    @pl.when(step < 2)
    def _():
        first = step == 0
        left = jnp.where(first, west, kept(nb_ref[count - 1, 2] >= 0, prev_ref[0].astype(F32)))
        right = jnp.where(first, kept(nb_ref[0, 3] >= 0, next_ref[0].astype(F32)), east)
        wide = jnp.concatenate([left, tile_ref[0].astype(F32), right], axis=1)
        north = jnp.where(first, north_ref[:1], north_ref[count - 1 :])
        south = jnp.where(first, south_ref[:1], south_ref[count - 1 :])
        store_taps(lhs_ref, 0, with_halo(wide, north, south))
        for g in range(GROUPS):
            cots_ref[g * S : (g + 1) * S, :] = cot_ref[0, :, g * 4 * CU : (g + 1) * 4 * CU]

    top = step == 2

    @pl.when(step >= 2)
    def _():
        tile_at = lax.broadcasted_iota(jnp.int32, (count, PAIR), 0)

        def row(r, at):
            found = jnp.concatenate([rows_a_ref[r], rows_b_ref[r]], axis=0)
            left = jnp.where(tile_at == 0, west[at : at + 1], found[:, :PAIR])
            right = jnp.where(tile_at == count - 1, east[at : at + 1], found[:, PW - PAIR :])
            return jnp.concatenate([left, found[:, PAIR : PW - PAIR], right], axis=1)

        edge = jnp.where(top, row(0, 0), row(3, S - 1))
        inner = jnp.where(top, row(1, 1), row(2, S - 2))
        above = jnp.where(top, north_ref[...], inner)
        below = jnp.where(top, inner, south_ref[...])
        store_taps(lhs_ref, 0, (above.astype(BF), edge.astype(BF), below.astype(BF)))
        cot = jnp.where(
            top,
            jnp.concatenate([cot_a_ref[0], cot_b_ref[0]], axis=0),
            jnp.concatenate([cot_a_ref[1], cot_b_ref[1]], axis=0),
        ).astype(BF)
        for g in range(GROUPS):
            cots_ref[g * S : (g + 1) * S, :] = cot[:, g * 4 * CU : (g + 1) * 4 * CU]

    conv = jnp.dot(lhs_ref[...], band_ref[...], preferred_element_type=F32)
    up = jnp.dot(cots_ref[...], wide_ref[...], preferred_element_type=F32)
    hidden, delta = activate(conv, up, half_scale_ref[...], half_shift_ref[...], scale_ref[...])
    at = lax.broadcasted_iota(jnp.int32, hidden.shape, 0) & (S - 1)
    ok = ((at > 0) & (at < count - 1)) | (step < 2)
    rounded = delta.astype(BF)
    hidden = kept(ok, hidden).astype(BF)
    add_conv(conv_acc, lhs_ref[...], kept(ok, delta).astype(BF))
    for j in range(4):
        expand_acc[...] += lax.dot_general(
            hidden[:, j * C : (j + 1) * C], cots_ref[:, j * CU : (j + 1) * CU], CONTRACT, preferred_element_type=F32
        )

    @pl.when(step < 2)
    def _():
        for g in range(GROUPS):
            delta_ref[0, :, g * GW : (g + 1) * GW] = rounded[g * S : (g + 1) * S]

    @pl.when(step == 0)
    def _():
        up_ref[:, W:] = rounded[:S, :PAIR]

    @pl.when(step == 1)
    def _():
        down_ref[:, W:] = rounded[(GROUPS - 1) * S :, GW - PAIR :]

    def rows_out(sent_ref, own_ref):
        for g in range(GROUPS):
            sent_ref[:, g * GW : (g + 1) * GW] = rounded[g * S : (g + 1) * S]
            own_ref[:, g * GW : (g + 1) * GW] = rounded[g * S : (g + 1) * S].astype(F32)

    @pl.when(step == 2)
    def _():
        rows_out(up_ref, up_own_ref)

    @pl.when(step == 3)
    def _():
        rows_out(down_ref, down_own_ref)
        expand_ref[...] = expand_acc[...]
        finish_conv(conv_acc, conv_in_ref, conv_ref)


def backward_kernel(
    base, nb_ref, field_ref, prev_ref, next_ref, north_ref, south_ref, west_ref, east_ref, top_ref, bottom_ref, band_ref, *rest
):
    out_ref, lhs_ref = rest[-2:]
    step = pl.program_id(0) + base
    count = nb_ref.shape[0]
    per = GROUPS * S

    def mended(value, tile, lanes):
        place = lax.broadcasted_iota(jnp.int32, value.shape, 0)
        value = jnp.where(place == 0, top_ref[pl.ds(tile, 1), :][:, lanes], value.astype(F32))
        return jnp.where(place == S - 1, bottom_ref[pl.ds(tile, 1), :][:, lanes], value)

    for k in range(TB):
        tile = step * TB + k
        left = field_ref[k - 1, :, W - PAIR :] if k > 0 else prev_ref[0]
        right = field_ref[k + 1, :, :PAIR] if k < TB - 1 else next_ref[0]
        left = mended(left, jnp.maximum(tile - 1, 0), slice(W - PAIR, W))
        right = mended(right, jnp.minimum(tile + 1, count - 1), slice(0, PAIR))
        if k == 0:
            left = jnp.where(tile == 0, west_ref[...].astype(F32), left)
        if k == TB - 1:
            right = jnp.where(tile == count - 1, east_ref[...].astype(F32), right)
        left = kept(nb_ref[tile, 2] >= 0, left)
        right = kept(nb_ref[tile, 3] >= 0, right)
        wide = jnp.concatenate([left, mended(field_ref[k], tile, slice(0, W)), right], axis=1)
        taps = with_halo(wide, north_ref[pl.ds(tile, 1), :], south_ref[pl.ds(tile, 1), :])
        store_taps(lhs_ref, k * per, taps)
    for k in range(TB):
        rows = slice(k * per, (k + 1) * per)
        grad = jnp.dot(lhs_ref[rows, :], band_ref[...], preferred_element_type=F32).astype(BF)
        for g in range(GROUPS):
            out_ref[k, :, g * GW : (g + 1) * GW] = grad[g * S : (g + 1) * S]


def field_specs(count, base):
    last = W // PAIR - 1
    return [
        pl.BlockSpec((TB, S, W), lambda i, nb: (i + base, 0, 0)),
        pl.BlockSpec((1, S, PAIR), lambda i, nb: (jnp.maximum((i + base) * TB - 1, 0), 0, last)),
        pl.BlockSpec((1, S, PAIR), lambda i, nb: (jnp.minimum((i + base) * TB + TB, count - 1), 0, 0)),
    ]


def whole(*shape):
    return pl.BlockSpec(shape, lambda i, nb: (0,) * len(shape))


ANY = pl.BlockSpec(memory_space=pl.ANY)
PARAMS = pltpu.CompilerParams(dimension_semantics=("arbitrary",), vmem_limit_bytes=44 * 2**20)
CONSTANTS = ((3 * KW, GW), (4 * CU, GW), (1, GW), (1, GW), (1, GW))
GRADS = ((9, C, C), (C, CU))


def halo_specs(count):
    return [whole(count, PW), whole(count, PW), whole(S, PAIR), whole(S, PAIR)]


def forward(tiles, cotangent, neighbours, constants, base, steps, grads, before=None):
    count = tiles.shape[0]
    rows = TB * GROUPS * S
    more = [] if before is None else [before]
    return pl.pallas_call(
        functools.partial(forward_kernel, base),
        grid_spec=pltpu.PrefetchScalarGridSpec(
            num_scalar_prefetch=1,
            grid=(steps,),
            in_specs=[
                *field_specs(count, base),
                pl.BlockSpec((TB, S, S * CU), lambda i, nb: (i + base, 0, 0)),
                *[whole(*shape) for shape in CONSTANTS + GRADS],
                *[ANY for _ in more],
            ],
            out_specs=[
                pl.BlockSpec((TB, S, W), lambda i, nb: (i + base, 0, 0)),
                whole(4, steps * TB, PW),
                whole(2, steps * TB, S * CU),
                *[whole(*shape) for shape in GRADS],
            ],
            scratch_shapes=[
                pltpu.VMEM((rows, 3 * KW), BF),
                pltpu.VMEM((3 * KW, GW), F32),
                pltpu.VMEM((C, CU), F32),
                pltpu.VMEM((rows, GW), BF),
                pltpu.VMEM((rows, GW), BF),
            ],
        ),
        out_shape=[
            jax.ShapeDtypeStruct((count, S, W), BF),
            jax.ShapeDtypeStruct((4, steps * TB, PW), F32),
            jax.ShapeDtypeStruct((2, steps * TB, S * CU), F32),
            *[jax.ShapeDtypeStruct(shape, F32) for shape in GRADS],
        ],
        input_output_aliases={12: 0} if more else {},
        compiler_params=PARAMS,
        cost_estimate=pl.CostEstimate(flops=steps * 2**32, bytes_accessed=steps * 3 * 2**20, transcendentals=0),
        name=f"forward_{base}",
    )(neighbours, tiles, tiles, tiles, cotangent, *constants, *grads, *more)


def edges(tiles, cotangent, neighbours, kept_rows, halos, constants, grads, delta):
    count = tiles.shape[0]
    ends = count - 1
    (rows_a, cot_a), (rows_b, cot_b) = kept_rows
    own = (count, W)
    sent = (count, W + PAIR)
    return pl.pallas_call(
        edge_kernel,
        grid_spec=pltpu.PrefetchScalarGridSpec(
            num_scalar_prefetch=1,
            grid=(4,),
            in_specs=[
                pl.BlockSpec((1, S, W), lambda i, nb: (ends * jnp.minimum(i, 1), 0, 0)),
                pl.BlockSpec((1, S, PAIR), lambda i, nb: (ends - 1, 0, W // PAIR - 1)),
                pl.BlockSpec((1, S, PAIR), lambda i, nb: (1, 0, 0)),
                pl.BlockSpec((1, S, S * CU), lambda i, nb: (ends * jnp.minimum(i, 1), 0, 0)),
                *[whole(*value.shape) for value in (rows_a, rows_b, cot_a, cot_b)],
                *halo_specs(count),
                *[whole(*shape) for shape in CONSTANTS + GRADS],
                ANY,
            ],
            out_specs=[
                pl.BlockSpec((1, S, W), lambda i, nb: (ends * jnp.minimum(i, 1), 0, 0)),
                whole(*sent), whole(*sent), whole(*own), whole(*own),
                *[whole(*shape) for shape in GRADS],
            ],
            scratch_shapes=[
                pltpu.VMEM((GROUPS * S, 3 * KW), BF),
                pltpu.VMEM((GROUPS * S, 4 * CU), BF),
                pltpu.VMEM((3 * KW, GW), F32),
                pltpu.VMEM((C, CU), F32),
            ],
        ),
        out_shape=[
            jax.ShapeDtypeStruct((count, S, W), BF),
            jax.ShapeDtypeStruct(sent, BF),
            jax.ShapeDtypeStruct(sent, BF),
            jax.ShapeDtypeStruct(own, F32),
            jax.ShapeDtypeStruct(own, F32),
            *[jax.ShapeDtypeStruct(shape, F32) for shape in GRADS],
        ],
        input_output_aliases={20: 0},
        compiler_params=PARAMS,
        cost_estimate=pl.CostEstimate(flops=2**33, bytes_accessed=2**22, transcendentals=0),
        name="edges",
    )(neighbours, tiles, tiles, tiles, cotangent, rows_a, rows_b, cot_a, cot_b, *halos, *constants, *grads, delta)


def backward(delta, halos, own, neighbours, bands, base, steps, before=None):
    count = delta.shape[0]
    rows = TB * GROUPS * S
    more = [] if before is None else [before]
    return pl.pallas_call(
        functools.partial(backward_kernel, base),
        grid_spec=pltpu.PrefetchScalarGridSpec(
            num_scalar_prefetch=1,
            grid=(steps,),
            in_specs=[
                *field_specs(count, base), *halo_specs(count), whole(count, W), whole(count, W), whole(3 * KW, GW),
                *[ANY for _ in more],
            ],
            out_specs=pl.BlockSpec((TB, S, W), lambda i, nb: (i + base, 0, 0)),
            scratch_shapes=[pltpu.VMEM((rows, 3 * KW), BF)],
        ),
        out_shape=jax.ShapeDtypeStruct((count, S, W), BF),
        input_output_aliases={11: 0} if more else {},
        compiler_params=PARAMS,
        cost_estimate=pl.CostEstimate(flops=steps * 2**31, bytes_accessed=steps * 2**20, transcendentals=0),
        name=f"backward_{base}",
    )(neighbours, delta, delta, delta, *halos, *own, bands, *more)


def swapped(value, move):
    cells = [(x, z, y, c) for x in range(4) for z in range(4) for y in range(4) for c in range(2)]
    number = {cell: i for i, cell in enumerate(cells)}
    return lax.ppermute(value, AXES, [(number[cell], number[move(cell)]) for cell in cells])


def flip(axis, second):
    def move(cell):
        there = list(cell)
        there[axis] = 3 - cell[axis] if second else cell[axis] ^ 1
        return tuple(there)

    return move


def tied(*values):
    return lax.optimization_barrier(values)


def local(tiles, cotangent, neighbours, conv_weight, expand_weight, norm_scale, norm_shift):
    count = tiles.shape[0]
    position = lax.axis_index("space")
    kernel = conv_weight.reshape(3, 3, C, C)
    flipped = jnp.transpose(jnp.flip(kernel, (0, 1)), (0, 1, 3, 2))
    turned = expand_weight.T
    wide = jnp.concatenate([jnp.pad(turned, ((CU * j, CU * (3 - j)), (0, 0))) for j in range(4)], axis=1)
    scale = jnp.tile(norm_scale, 4)[None]
    half_shift = 0.5 * jnp.tile(norm_shift, 4)[None]
    constants = (band(kernel), wide, 0.5 * scale, half_shift, scale)
    down = jnp.concatenate([tiles[:, S - 1], tiles[count - 1, :, W - PAIR :]], axis=1)
    up = jnp.concatenate([tiles[:, 0], tiles[0, :, :PAIR]], axis=1)
    blocks = count // TB
    early = blocks // 2

    near = halo_near(down, up)
    grads = tuple(jnp.zeros(shape, F32) for shape in GRADS)
    delta, *first_rows, conv_part, expand_part = forward(tiles, cotangent, neighbours, constants, 0, early, grads)
    near, delta = tied(near, delta)
    far = halo_far(down, up, near)
    delta, *last_rows, conv_part, expand_part = forward(
        tiles, cotangent, neighbours, constants, early, blocks - early, (conv_part, expand_part), delta
    )
    far, delta = tied(far, delta)
    halos = halo(down, up, near, far, neighbours, position)
    delta, up, down, top, bottom, conv_part, expand_part = edges(
        tiles, cotangent, neighbours, (first_rows, last_rows), halos, constants, (conv_part, expand_part), delta
    )

    part = jnp.concatenate([conv_part.reshape(9 * 32, 2 * C), expand_part.reshape(2 * C, 2 * C)], axis=0)
    half = part.shape[0] // 2
    even = lax.axis_index("space") % 2 == 0
    low, high = part[:half], part[half:]
    near = halo_near(down, up)
    other = swapped(jnp.where(even, high, low), flip(3, False))
    part = jnp.where(even, low, high) + other
    far = halo_far(down, up, near)
    back = band(flipped)
    grad = None
    counts = [blocks * (i + 1) // PIECES - blocks * i // PIECES for i in range(PIECES)]
    halos = None
    for turn in range(6):
        other = swapped(part, flip(turn // 2, turn % 2 == 1))
        piece = turn - (6 - PIECES)
        if piece >= 0:
            if halos is None:
                halos = halo(down, up, near, far, neighbours, position)
            grad = backward(delta, halos, (top, bottom), neighbours, back, sum(counts[:piece]), counts[piece], grad)
            other, grad = tied(other, grad)
        part = part + other
        if grad is not None:
            part, grad = tied(part, grad)
    other = swapped(part, flip(3, False))
    total = jnp.concatenate([jnp.where(even, part, other), jnp.where(even, other, part)], axis=0)
    cells = lax.axis_size("dp") * lax.axis_size("space") * count * S * S
    total = total * (1.0 / math.sqrt(cells))
    return grad, total[: 9 * 32].reshape(9, C * C), total[9 * 32 :].reshape(C, CU)


def solution(mesh):
    placed = (P(AXES, None, None), P(AXES, None, None), P(AXES, None), P(), P(), P(), P())
    return jax.shard_map(
        local,
        mesh=mesh,
        in_specs=placed,
        out_specs=(P(AXES, None, None), P(), P()),
        check_vma=False,
    )
```
